32 devices in a mesh: members: 4 (over y, x), rows: 2 (over core), cols: 4 (over z).
Axes of the slice: x: 2, y: 2, z: 4, core: 2. Of those that a mesh axis runs over, the one named last changes fastest.
Arguments:
- ensemble: bfloat16 [80, 64, 128, 128], P('members', 'rows', 'cols'), may hold values from -6 to 6
- measured_brightness: float32 [16384, 16], P(('rows', 'cols')), may hold values from -6 to 6
- obs_rinv: float32 [16384, 16], P(('rows', 'cols')), may hold values from 0.05 to 1
- obs_tile: int32 [16384, 1], P(('rows', 'cols')), may hold values from 0 to 7; in each aligned block of 2048 rows (0 to 2047, 2048 to 4095, ...) at most 512 rows name the same one
- footprint: int32 [16384, 4], P(('rows', 'cols')), may hold values from 0 to 1443
- obs_shift: int32 [16384, 1], P(('rows', 'cols')), may hold values from 0 to 15
- chan_base: int32 [16], replicated, may hold values from 0 to 8
- band_weights: float32 [16, 4, 8], replicated, may hold values from -1 to 1
Outputs:
- analysis: bfloat16 [80, 64, 128, 128], P('members', 'rows', 'cols')
The draws below stay inside these ranges and needn't reach their ends.
Inputs may be any that keep to these rules, and one draw needn't show every extreme that they name: `obs_tile`: within the rows held by one tile position, at most 512 profiles name any one tile, and 512 is reached; every tile is named somewhere.
All inputs are finite; a program needn't handle non-finite values.
Results may differ from the reference program's by a relative error of at most 0.0065.
Values may be sent and summed in bfloat16 or wider, within the bound.
A program may use at most 192 MiB of HBM per device.

```python
import math
import jax
import jax.numpy as jnp
import numpy as np
from jax import lax

TRIAL_STATES = 80
FIELDS = 4
LEV = 32
SPECTRAL_BANDS = 16
BAND = 8
SHIFTS = 16
FP = 4
HW = 3
ITERS = 8
CR = 32
CC = 32
OBS_DEV = 2048
VARS = 128
TILES = 8
CAP = 512
NR = 64
NC = 128
NOBS = 16384
N_ROWS = 2
N_COLS = 4


def with_ends(array, rng, smallest, high):
    index_at = [jax.random.randint(jax.random.fold_in(rng, axis), (), 0, length) for axis, length in enumerate(array.shape)]
    main_axis = array.shape.index(max(array.shape))
    next_to = index_at[:main_axis] + [(index_at[main_axis] + 1) % array.shape[main_axis]] + index_at[main_axis + 1:]
    return array.at[tuple(index_at)].set(smallest).at[tuple(next_to)].set(high)


def block_scale(own_key, dims, pieces, low, largest):
    def one(dim, shards_of):
        heights = jax.random.uniform(jax.random.fold_in(jax.random.fold_in(own_key, 6), dim), (shards_of,), jnp.float32, low / len(pieces), largest / len(pieces))
        return jnp.repeat(jnp.exp(heights), dims[dim] // shards_of).reshape((-1,) + (1,) * (len(dims) - dim - 1))

    factor_of = one(*pieces[0])
    for cut in pieces[1:]:
        factor_of = factor_of * one(*cut)
    return factor_of


def deal_out(key, own, number, rows, number_of, top, limit, skew):
    ranking = jax.random.permutation(key, number_of)
    heavy_load, ordinary = portions_of(number_of, rows * top, limit, skew, True), portions_of(number_of, rows * top, limit, skew, False)
    places = jnp.arange(number_of)

    def named(tallies, rotation):
        used = int((tallies > 0).sum())
        fixed = max(1, used // 4)
        moved = fixed + (places - fixed + rotation * (used - fixed)) % max(1, number_of - fixed)
        return jnp.zeros((number_of,), jnp.int32).at[ranking[jnp.where(places < fixed, places, moved)]].set(jnp.asarray(tallies, jnp.int32))

    tallies = jnp.where(number % 4 == 0, named(heavy_load, number // 4), named(ordinary, number - number // 4 - 1))
    mixed = jax.random.permutation(jax.random.fold_in(own, 3), number_of)
    source_of, sink = mixed[0:number_of // 2 * 2:2], mixed[1:number_of // 2 * 2:2]
    margin = jnp.minimum(tallies[source_of] - 1, limit - tallies[sink]) // 2
    margin = jnp.where((source_of == ranking[0]) | (sink == ranking[0]) | (tallies[sink] == 0), 0, jnp.maximum(margin, 0))
    moved = jax.random.randint(jax.random.fold_in(own, 4), (number_of // 2,), 0, 1 << 20) % (margin + 1)
    tallies = tallies.at[source_of].add(-moved).at[sink].add(moved)
    items = jnp.searchsorted(jnp.cumsum(tallies), jnp.arange(rows * top), side="right").astype(jnp.int32)
    grid = items.reshape(top, rows).T
    grid = grid[jax.random.permutation(jax.random.fold_in(own, 1), rows)]
    rotation = jax.random.randint(jax.random.fold_in(own, 2), (rows, 1), 0, top)
    return jnp.take_along_axis(grid, (jnp.arange(top)[None, :] + rotation) % top, axis=1)


def portions_of(amount, total, most, lean, full):
    loads = [(1 << 20) // math.isqrt(grade ** lean) + 1 for grade in range(1, amount + 1)]
    largest = most if full else min(most, max(-(-total // amount), total * loads[0] // sum(loads)))
    least = 1 if total - largest >= amount - 1 else 0
    counts, spare = [largest] + [least] * (amount - 1), total - largest - least * (amount - 1)
    while spare > 0:
        movable = [i for i in range(1, amount) if counts[i] < largest] or [i for i in range(1, amount) if counts[i] < most]
        mass, budget = sum([loads[i] for i in movable]), spare
        for i in movable:
            extra = min(most - counts[i], max(1, budget * loads[i] // mass), spare)
            counts[i] = counts[i] + extra
            spare = spare - extra
    return np.array(counts)


def centred(stream_key, extent, scale, limit, cuts=(), held_as=jnp.bfloat16):
    array = jax.random.normal(stream_key, extent, jnp.float32) * scale
    if len(cuts) > 0:
        array = block_scale(stream_key, extent, cuts, -0.22, 0.18) * array
    return jnp.clip(array, min=-limit, max=limit).astype(held_as)


def setup_inputs(seed: int = 0) -> dict:
    keys = jax.random.split(jax.random.key(seed), 9)
    ensemble = centred(keys[0], (TRIAL_STATES, NR, NC, VARS), 1.0, 6.0, ((0, 4), (1, 2), (2, 4)))
    measured_brightness = centred(keys[1], (NOBS, SPECTRAL_BANDS), 1.0, 6.0, ((0, 8),), jnp.float32)
    obs_rinv = jnp.clip(jnp.exp(math.log(1.0) - 2.9957323 * jax.random.uniform(keys[2], (NOBS, SPECTRAL_BANDS), jnp.float32) ** block_scale(keys[2], (NOBS, SPECTRAL_BANDS), ((0, 8),), -0.2, 0.2)), 0.05, 1.0)
    obs_tile_keys = jax.random.split(jax.random.fold_in(keys[3], 1), NOBS // OBS_DEV)
    obs_tile_turns = jax.random.permutation(jax.random.fold_in(keys[3], 3), NOBS // OBS_DEV)
    obs_tile = jax.vmap(lambda own, number: deal_out(jax.random.fold_in(keys[3], 2), own, number, OBS_DEV, TILES, 1, CAP, 2))(obs_tile_keys, obs_tile_turns).reshape((NOBS, 1))
    footprint = with_ends(jax.random.randint(keys[4], (NOBS, FP), 0, (CR + 2 * HW) * (CC + 2 * HW)), jax.random.fold_in(keys[4], 1), 0, ((CR + 2 * HW) * (CC + 2 * HW)) - 1).astype(jnp.int32)
    obs_shift = with_ends(jax.random.randint(keys[5], (NOBS, 1), 0, SHIFTS), jax.random.fold_in(keys[5], 1), 0, SHIFTS - 1).astype(jnp.int32)
    chan_base = with_ends(jax.random.randint(keys[6], (SPECTRAL_BANDS,), 0, LEV - BAND - SHIFTS + 1), jax.random.fold_in(keys[6], 1), 0, LEV - BAND - SHIFTS).astype(jnp.int32)
    band_weights = centred(keys[7], (SPECTRAL_BANDS, FIELDS, BAND), (FIELDS * BAND) ** -0.5, 1.0, (), jnp.float32)
    return {"ensemble": ensemble, "measured_brightness": measured_brightness, "obs_rinv": obs_rinv, "obs_tile": obs_tile, "footprint": footprint, "obs_shift": obs_shift, "chan_base": chan_base, "band_weights": band_weights}


maximum_element = lax.Precision.HIGHEST

def band_matrix(shift_rows, chan_base, band_weights):
    levels = jnp.arange(LEV, dtype=jnp.int32)
    start_level = chan_base[None, :] + shift_rows[:, None]
    offset = levels[None, None, :] - start_level[:, :, None]
    band_total = jnp.zeros((shift_rows.shape[0], SPECTRAL_BANDS, FIELDS, LEV), jnp.float32)
    for layer in range(BAND):
        hit_mask = (offset == layer).astype(jnp.float32)
        band_total = band_total + band_weights[None, :, :, layer, None] * hit_mask[:, :, None, :]
    return band_total.reshape(shift_rows.shape[0], SPECTRAL_BANDS, FIELDS * LEV)

def square_root_transform(gram_matrix, drive_vector):
    frobenius = jnp.sqrt(jnp.sum(gram_matrix * gram_matrix))
    identity = jnp.eye(TRIAL_STATES, dtype=jnp.float32)
    approach = gram_matrix / frobenius
    inverse = identity
    for sweep_index in range(ITERS):
        factor = 1.5 * identity - 0.5 * jnp.dot(inverse, approach, precision=maximum_element)
        approach = jnp.dot(approach, factor, precision=maximum_element)
        inverse = jnp.dot(factor, inverse, precision=maximum_element)
    spread_weights = jnp.sqrt((TRIAL_STATES - 1) / frobenius) * inverse
    mean_weights = jnp.dot(inverse, jnp.dot(inverse, drive_vector, precision=maximum_element), precision=maximum_element) / frobenius
    return spread_weights + mean_weights[:, None]

def reference(ensemble, measured_brightness, obs_rinv, obs_tile, footprint, obs_shift, chan_base, band_weights):
    tile_count = N_ROWS * N_COLS
    incoming_payload = 2 * OBS_DEV
    panel_rows = CR + 2 * HW
    panel_cols = CC + 2 * HW
    mean_state = lax.optimization_barrier(jnp.sum(ensemble.astype(jnp.float32), axis=0)) / TRIAL_STATES
    mean_rounded = mean_state.astype(jnp.bfloat16)
    perturb = (ensemble.astype(jnp.float32) - mean_state[None]).astype(jnp.bfloat16)
    stacked = jnp.concatenate([perturb, mean_rounded[None]], axis=0)
    padded = jnp.pad(stacked, ((0, 0), (HW, HW), (HW, HW), (0, 0)))
    destination = obs_tile[:, 0]

    def one_tile(tile_id):
        tile_row = (tile_id // N_COLS).astype(jnp.int32)
        tile_col = (tile_id % N_COLS).astype(jnp.int32)
        zero_index = jnp.int32(0)
        tile_panel = lax.dynamic_slice(padded, (zero_index, tile_row * CR, tile_col * CC, zero_index), (TRIAL_STATES + 1, panel_rows, panel_cols, VARS))
        panel_flat = tile_panel.reshape(TRIAL_STATES + 1, panel_rows * panel_cols, VARS)
        member_of = destination == tile_id
        chosen_elements = jnp.nonzero(member_of, size=incoming_payload, fill_value=0)[0].astype(jnp.int32)
        obs_count = jnp.sum(member_of.astype(jnp.int32))
        live_mask = (jnp.arange(incoming_payload, dtype=jnp.int32) < obs_count).astype(jnp.float32)
        gridpoint_number = footprint[chosen_elements]
        shifts = obs_shift[chosen_elements, 0]
        gathered = jnp.take(panel_flat, gridpoint_number.reshape(-1), axis=1).astype(jnp.float32)
        gathered = gathered.reshape(TRIAL_STATES + 1, incoming_payload, FP, VARS)
        nearby_average = lax.optimization_barrier(jnp.sum(gathered, axis=2)) * (1.0 / FP)
        measurement_mapping = band_matrix(shifts, chan_base, band_weights)
        background_guess = jnp.einsum('wnf,nrf->wnr', nearby_average, measurement_mapping, precision=maximum_element)
        quantized_measurements = lax.optimization_barrier(background_guess[:TRIAL_STATES].astype(jnp.bfloat16))
        perturbed_observations = quantized_measurements.astype(jnp.float32).reshape(TRIAL_STATES, incoming_payload * SPECTRAL_BANDS)
        misfit_list = (measured_brightness[chosen_elements] - background_guess[TRIAL_STATES]).reshape(-1)
        weight = (obs_rinv[chosen_elements] * live_mask[:, None]).reshape(-1)
        weighted = perturbed_observations * weight[None, :]
        gram_matrix = (TRIAL_STATES - 1) * jnp.eye(TRIAL_STATES, dtype=jnp.float32) + jnp.dot(weighted, perturbed_observations.T, precision=maximum_element)
        drive_vector = jnp.dot(weighted, misfit_list, precision=maximum_element)
        coeff = square_root_transform(gram_matrix, drive_vector)
        tile_block = lax.dynamic_slice(stacked, (zero_index, tile_row * CR, tile_col * CC, zero_index), (TRIAL_STATES + 1, CR, CC, VARS)).astype(jnp.float32)
        result = tile_block[TRIAL_STATES][None] + jnp.einsum('mrcv,mj->jrcv', tile_block[:TRIAL_STATES], coeff, precision=maximum_element)
        return result.astype(jnp.bfloat16)
    tiles_out = lax.map(one_tile, jnp.arange(tile_count, dtype=jnp.int32))
    shaped = tiles_out.reshape(N_ROWS, N_COLS, TRIAL_STATES, CR, CC, VARS).transpose(2, 0, 3, 1, 4, 5)
    return shaped.reshape(TRIAL_STATES, N_ROWS * CR, N_COLS * CC, VARS)
```

```python
import functools

import jax
import jax.numpy as jnp
from jax import lax
from jax.experimental import pallas as pl
from jax.experimental.pallas import tpu as pltpu
from jax.sharding import PartitionSpec as P

TRIAL_STATES = 80
FIELDS = 4
LEV = 32
SPECTRAL_BANDS = 16
BAND = 8
SHIFTS = 16
FP = 4
HW = 3
ITERS = 8
VARS = 128
CELLS = 8
CORNER = 16

bf16 = jnp.bfloat16
f32 = jnp.float32
HIGHEST = lax.Precision.HIGHEST
VMEM_LIMIT = 50 * 1024 * 1024
NT = (((1,), (1,)), ((), ()))


def shift_table(chan_base, band_weights):
    levels = jnp.arange(LEV, dtype=jnp.int32)
    shifts = jnp.arange(SHIFTS, dtype=jnp.int32)
    offset = levels[None, None, :] - (chan_base[None, :] + shifts[:, None])[:, :, None]
    total = jnp.zeros((SHIFTS, SPECTRAL_BANDS, FIELDS, LEV), f32)
    for layer in range(BAND):
        hit = offset == layer
        total = total + jnp.where(hit[:, :, None, :], band_weights[None, :, :, layer, None], 0.0)
    table = total.reshape(SHIFTS * SPECTRAL_BANDS, VARS)
    high = table.astype(bf16)
    low = (table - high.astype(f32)).astype(bf16)
    return jnp.concatenate([high, low], axis=1)


def obs_kernel(spots_ref, shift_ref, table_ref, own_ref, *refs):
    halo_refs, out_ref, spread = refs[:-2], refs[-2], refs[-1]
    slots = spots_ref.shape[0]
    cells = own_ref.shape[1] + sum(ref.shape[1] for ref in halo_refs)
    width = spread.shape[1]
    chunk = min(1024, slots)

    @pl.when(pl.program_id(0) == 0)
    def _():
        for start in range(0, slots, chunk):
            columns = lax.broadcasted_iota(jnp.int32, (chunk, width), 1)
            hits = jnp.zeros((chunk, width), f32)
            for q in range(FP):
                hits = hits + jnp.where(spots_ref[start:start + chunk, q:q + 1] == columns, 1.0 / FP, 0.0)
            spread[start:start + chunk, :] = hits.astype(bf16)

    panel = jnp.concatenate(
        [
            jnp.concatenate([own_ref[0], own_ref[1]], axis=1),
        ]
        + [jnp.concatenate([ref[0], ref[1]], axis=1) for ref in halo_refs]
        + [jnp.zeros((width - cells, 2 * VARS), bf16)] * (width > cells),
        axis=0,
    )
    for start in range(0, slots, chunk):
        average = jnp.dot(
            spread[start:start + chunk, :], panel, preferred_element_type=f32
        ).astype(bf16)
        shift = shift_ref[:, start:start + chunk]
        for k in range(2):
            part = average[:, k * VARS:(k + 1) * VARS]
            projected = lax.dot_general(
                table_ref[...],
                jnp.concatenate([part, part], axis=1),
                NT,
                preferred_element_type=f32,
            )
            picked = projected[:SPECTRAL_BANDS]
            for s in range(1, SHIFTS):
                picked = jnp.where(
                    shift == s, projected[s * SPECTRAL_BANDS:(s + 1) * SPECTRAL_BANDS], picked
                )
            out_ref[k, :, start:start + chunk] = picked.astype(out_ref.dtype)


def observe(spots, shifts, table, own, halo, pairs, dtype):
    slots = spots.shape[0]
    cells = own.shape[1] + sum(e.shape[1] for e in halo)
    width = cells + -cells % 256
    return pl.pallas_call(
        obs_kernel,
        grid=(pairs,),
        in_specs=[
            pl.BlockSpec((slots, FP), lambda i: (0, 0)),
            pl.BlockSpec((1, slots), lambda i: (0, 0)),
            pl.BlockSpec(table.shape, lambda i: (0, 0)),
        ]
        + [pl.BlockSpec((2, e.shape[1], VARS), lambda i: (i, 0, 0)) for e in [own] + halo],
        out_specs=pl.BlockSpec((2, SPECTRAL_BANDS, slots), lambda i: (i, 0, 0)),
        out_shape=jax.ShapeDtypeStruct((2 * pairs, SPECTRAL_BANDS, slots), dtype),
        scratch_shapes=[pltpu.VMEM((slots, width), bf16)],
        compiler_params=pltpu.CompilerParams(vmem_limit_bytes=VMEM_LIMIT),
        cost_estimate=pl.CostEstimate(
            flops=4 * pairs * slots * width * VARS,
            bytes_accessed=4 * pairs * width * VARS,
            transcendentals=0,
        ),
    )(spots, shifts, table, own, *halo)


def gram_kernel(trials, numbers_ref, fold_ref, *refs):
    obs_refs, out_ref, rows = refs[:-2], refs[-2], refs[-1]
    slots = numbers_ref.shape[1]
    root = jnp.sqrt(numbers_ref[SPECTRAL_BANDS:, :])
    size = trials * SPECTRAL_BANDS
    for q, ref in enumerate(obs_refs):
        obs = ref[:trials].astype(bf16).astype(f32)
        rows[q * size:(q + 1) * size, :] = (
            (obs * root[None]).reshape(size, slots).astype(bf16)
        )
    departure = (numbers_ref[:SPECTRAL_BANDS, :] - obs_refs[0][trials]) * root
    high = departure.astype(bf16)
    base = len(obs_refs) * size
    rows[base:base + SPECTRAL_BANDS, :] = high
    rows[base + SPECTRAL_BANDS:, :] = (departure - high.astype(f32)).astype(bf16)
    total_rows = rows.shape[0]
    folded = jnp.zeros((fold_ref.shape[0], total_rows), f32)
    edges = list(range(0, base, size)) + [base, total_rows]
    for start, end in zip(edges[:-1], edges[1:]):
        full = lax.dot_general(rows[start:end, :], rows[...], NT, preferred_element_type=f32)
        r = lax.broadcasted_iota(jnp.int32, full.shape, 0) & (SPECTRAL_BANDS - 1)
        c = lax.broadcasted_iota(jnp.int32, full.shape, 1) & (SPECTRAL_BANDS - 1)
        full = jnp.where(r == c, full, 0.0)
        high = full.astype(bf16)
        low = (full - high.astype(f32)).astype(bf16)
        fold = fold_ref[:, start:end]
        folded = folded + jnp.dot(fold, high, preferred_element_type=f32)
        folded = folded + jnp.dot(fold, low, preferred_element_type=f32)
    high = folded.astype(bf16)
    low = (folded - high.astype(f32)).astype(bf16)
    out_ref[...] = lax.dot_general(
        high, fold_ref[...], NT, preferred_element_type=f32
    ) + lax.dot_general(low, fold_ref[...], NT, preferred_element_type=f32)


def transform_kernel(gram_ref, order_ref, high_ref, low_ref):
    both = gram_ref[...]
    r = lax.broadcasted_iota(jnp.int32, both.shape, 0)
    c = lax.broadcasted_iota(jnp.int32, both.shape, 1)
    identity = jnp.where(r == c, 1.0, 0.0)
    inside = (r < TRIAL_STATES) & (c < TRIAL_STATES)
    gram = jnp.where(inside, both + (TRIAL_STATES - 1) * identity, 0.0)
    drive = jnp.where((r == TRIAL_STATES) & (c < TRIAL_STATES), both, 0.0)
    frobenius = jnp.sqrt(jnp.sum(gram * gram, keepdims=True))
    approach = gram / frobenius
    inverse = identity
    for sweep in range(ITERS):
        if sweep == 0:
            factor = 1.5 * identity - 0.5 * approach
            inverse = factor
        else:
            factor = 1.5 * identity - 0.5 * jnp.dot(inverse, approach, precision=HIGHEST)
            inverse = jnp.dot(factor, inverse, precision=HIGHEST)
        if sweep < ITERS - 1:
            approach = jnp.dot(approach, factor, precision=HIGHEST)
    weights = jnp.dot(jnp.dot(drive, inverse, precision=HIGHEST), inverse, precision=HIGHEST)
    weights = jnp.sum(weights, axis=0, keepdims=True) / frobenius
    coeff = jnp.sqrt((TRIAL_STATES - 1) / frobenius) * inverse + weights
    rows = TRIAL_STATES * CELLS
    r = lax.broadcasted_iota(jnp.int32, (rows, both.shape[1]), 0)
    c = lax.broadcasted_iota(jnp.int32, (rows, both.shape[1]), 1)
    expand = jnp.where(lax.shift_right_logical(r, 3) == c, 1.0, 0.0).astype(bf16)
    r = lax.broadcasted_iota(jnp.int32, (rows, rows), 0) & (CELLS - 1)
    c = lax.broadcasted_iota(jnp.int32, (rows, rows), 1) & (CELLS - 1)
    same = r == c
    high = coeff.astype(bf16)
    low = (coeff - high.astype(f32)).astype(bf16)
    for part, ref in ((high, high_ref), (low, low_ref)):
        tall = jnp.dot(expand, part, preferred_element_type=f32).astype(bf16)
        wide = lax.dot_general(tall, order_ref[...], NT, preferred_element_type=f32)
        ref[...] = jnp.where(same, wide, 0.0).astype(bf16)


def mix_kernel(dest_ref, high_ref, low_ref, mean_ref, *refs):
    parts, out_ref = refs[:-1], refs[-1]
    trials, cells = out_ref.shape[0], out_ref.shape[1]
    mean = mean_ref[...]
    rounded = mean.astype(bf16).astype(f32)
    for start in range(0, cells, 2 * CELLS):
        sides = []
        for half in range(2):
            at = start + half * CELLS
            block = [
                (ref[:, start:start + 2 * CELLS, :].astype(f32)[:, half * CELLS:(half + 1) * CELLS, :]
                 - mean[None, at:at + CELLS, :]).reshape(trials * CELLS, VARS).astype(bf16)
                for ref in parts
            ]
            sides.append(jnp.concatenate(block, axis=0))
        x = jnp.concatenate(sides, axis=1)
        y = jnp.dot(high_ref[0], x, preferred_element_type=f32)
        y = y + jnp.dot(low_ref[0], x, preferred_element_type=f32)
        halves = [
            y[:, h * VARS:(h + 1) * VARS].reshape(trials, CELLS, VARS)
            + rounded[None, start + h * CELLS:start + (h + 1) * CELLS, :]
            for h in range(2)
        ]
        out_ref[:, start:start + 2 * CELLS, :] = jnp.concatenate(halves, axis=1).astype(bf16)


def mix(dest, high, low, mean, parts):
    trials, cells, _ = parts[0].shape
    block = min(64, cells)
    spec = pl.BlockSpec((trials, block, VARS), lambda i, d: (0, i, 0))
    kron_spec = pl.BlockSpec((1,) + high.shape[1:], lambda i, d: (d[0], 0, 0))
    return pl.pallas_call(
        mix_kernel,
        grid_spec=pltpu.PrefetchScalarGridSpec(
            num_scalar_prefetch=1,
            grid=(cells // block,),
            in_specs=[kron_spec, kron_spec, pl.BlockSpec((block, VARS), lambda i, d: (i, 0))]
            + [spec] * len(parts),
            out_specs=spec,
        ),
        out_shape=jax.ShapeDtypeStruct(parts[0].shape, bf16),
        compiler_params=pltpu.CompilerParams(vmem_limit_bytes=VMEM_LIMIT),
        cost_estimate=pl.CostEstimate(
            flops=4 * high.shape[1] * high.shape[2] * cells * VARS // CELLS,
            bytes_accessed=2 * (len(parts) + 1) * trials * cells * VARS,
            transcendentals=0,
        ),
    )(dest[None], high, low, mean, *parts)


def route(measured, rinv, obs_tile, footprint, obs_shift, tile_count, rows, cols):
    count = measured.shape[0]
    capacity = 2 * count // tile_count
    dest = obs_tile[:, 0]
    onehot = (jnp.arange(tile_count, dtype=jnp.int32)[:, None] == dest[None, :]).astype(bf16)
    lanes = 128
    groups = count // lanes
    grouped = onehot.reshape(tile_count, groups, lanes)
    upper = (jnp.arange(lanes)[:, None] < jnp.arange(lanes)[None, :]).astype(bf16)
    within = jnp.einsum("tbi,ij->tbj", grouped, upper, preferred_element_type=f32)
    sums = jnp.sum(grouped.astype(f32), axis=2)
    earlier = (jnp.arange(groups)[:, None] < jnp.arange(groups)[None, :]).astype(f32)
    offset = jnp.einsum("tb,bc->tc", sums, earlier, precision=HIGHEST)
    place = jnp.sum((within + offset[:, :, None]) * grouped.astype(f32), axis=0).reshape(count)
    slot = dest * capacity + place.astype(jnp.int32)
    wide = cols + 2 * HW
    i = footprint // wide
    j = footprint - i * wide
    ii, jj = i - HW, j - HW
    top = rows * cols
    bottom = top + HW * cols
    left = bottom + HW * cols
    right = left + HW * rows
    corner = right + HW * rows
    spot = ii * cols + jj
    spot = jnp.where(ii < 0, top + i * cols + jj, spot)
    spot = jnp.where(ii >= rows, bottom + (ii - rows) * cols + jj, spot)
    outer = jnp.where(ii < 0, i, HW + ii - rows)
    middle = (ii >= 0) & (ii < rows)
    at_left = jnp.where(middle, left + j * rows + ii, corner + j * CORNER + outer)
    at_right = jnp.where(
        middle,
        right + (jj - cols) * rows + ii,
        corner + (HW + jj - cols) * CORNER + outer,
    )
    spot = jnp.where(jj < 0, at_left, jnp.where(jj >= cols, at_right, spot))
    payload = jnp.concatenate(
        [
            measured.T.astype(bf16),
            rinv.T.astype(bf16),
            (spot >> 6).T.astype(bf16),
            (spot & 63).T.astype(bf16),
            obs_shift.T.astype(bf16),
            jnp.zeros((7, count), bf16),
        ],
        axis=0,
    )
    table = (slot[:, None] == jnp.arange(tile_count * capacity, dtype=jnp.int32)[None, :]).astype(bf16)
    packed = jnp.dot(payload, table, preferred_element_type=f32).astype(bf16)
    packed = packed.reshape(-1, tile_count, capacity).transpose(1, 0, 2)
    got = lax.all_to_all(packed, ("rows", "cols"), split_axis=0, concat_axis=0, tiled=True)
    got = got.transpose(1, 0, 2).reshape(-1, tile_count * capacity).astype(f32)
    numbers = got[:2 * SPECTRAL_BANDS]
    at = 2 * SPECTRAL_BANDS
    spots = (got[at:at + FP] * 64.0 + got[at + FP:at + 2 * FP]).astype(jnp.int32).T
    shifts = got[at + 2 * FP:at + 2 * FP + 1].astype(jnp.int32)
    return numbers, spots, shifts


def neighbours(x_last, x_first, axis):
    peers = lax.axis_size(axis)
    up = [(i, i + 1) for i in range(peers - 1)]
    down = [(i + 1, i) for i in range(peers - 1)]
    return lax.ppermute(x_last, axis, up), lax.ppermute(x_first, axis, down)


def total_of(pieces, swap):
    got = [lax.ppermute(p, "members", swap[q]) if q else p for q, p in enumerate(pieces)]
    total = got[0]
    for piece in got[1:]:
        total = total + piece
    return total


def per_device(
    ensemble, measured_brightness, obs_rinv, obs_tile, footprint, obs_shift, chan_base, band_weights
):
    trials, rows, cols, _ = ensemble.shape
    members = lax.axis_size("members")
    me = lax.axis_index("members")
    tile_count = lax.axis_size("rows") * lax.axis_size("cols")
    cells = rows * cols
    share = cells // members
    swap = [[(i, i ^ q) for i in range(members)] for q in range(members)]
    order = list(range(members - 1, -1, -1))

    local = jnp.sum(ensemble.astype(f32), axis=0).reshape(cells, VARS)
    share_mean = total_of(
        [lax.dynamic_slice_in_dim(local, (me ^ q) * share, share, axis=0) for q in range(members)],
        swap,
    ) / TRIAL_STATES
    mean = jnp.zeros((cells, VARS), f32)
    for q in range(members):
        piece = lax.ppermute(share_mean, "members", swap[q]) if q else share_mean
        mean = lax.dynamic_update_slice_in_dim(mean, piece, (me ^ q) * share, axis=0)
    mean = mean.reshape(rows, cols, VARS)
    rounded = mean.astype(bf16)

    numbers, spots, shifts = route(
        measured_brightness, obs_rinv, obs_tile, footprint, obs_shift, tile_count, rows, cols
    )
    table = shift_table(chan_base, band_weights)

    perturb = (ensemble.astype(f32) - mean[None]).astype(bf16)
    spare = (trials + 1) % 2
    stacked = jnp.concatenate(
        [perturb, rounded[None]] + [jnp.zeros((spare, rows, cols, VARS), bf16)] * (spare > 0), axis=0
    )
    count = stacked.shape[0]
    before, after = neighbours(stacked[:, rows - HW:], stacked[:, :HW], "rows")
    left, right = neighbours(
        stacked[:, :, cols - HW:].transpose(0, 2, 1, 3), stacked[:, :, :HW].transpose(0, 2, 1, 3), "cols"
    )

    def corners(at):
        both = jnp.concatenate([before[:, :, at:at + HW], after[:, :, at:at + HW]], axis=1)
        both = both.transpose(0, 2, 1, 3)
        return jnp.pad(both, ((0, 0), (0, 0), (0, CORNER - 2 * HW), (0, 0)))

    corner_left, corner_right = neighbours(corners(cols - HW), corners(0), "cols")
    halo = [
        e.reshape(count, -1, VARS) for e in (before, after, left, right, corner_left, corner_right)
    ]
    own = stacked.reshape(count, cells, VARS)

    flat = ensemble.reshape(trials, cells, VARS)
    flat, _ = lax.optimization_barrier((flat, mean))
    parts = [None] * members
    for q in order:
        piece = lax.dynamic_slice_in_dim(flat, (me ^ q) * share, share, axis=1)
        parts[q] = piece if q == 0 else lax.ppermute(piece, "members", swap[q])

    slots = spots.shape[0] // members
    observed = [None] * members
    for q in order:
        at = (me ^ q) * slots
        result = observe(
            lax.dynamic_slice_in_dim(spots, at, slots, axis=0),
            lax.dynamic_slice_in_dim(shifts, at, slots, axis=1),
            table,
            own,
            halo,
            (trials + 1) // 2 if q else (trials + 2) // 2,
            bf16 if q else f32,
        )
        observed[q] = lax.ppermute(result[:trials], "members", swap[q]) if q else result

    total_rows = (TRIAL_STATES + 2) * SPECTRAL_BANDS
    member_at = jnp.arange(total_rows, dtype=jnp.int32) // SPECTRAL_BANDS
    true_at = ((member_at // trials) ^ me) * trials + member_at % trials
    true_at = jnp.where(member_at >= TRIAL_STATES, TRIAL_STATES, true_at)
    fold = (jnp.arange(128, dtype=jnp.int32)[:, None] == true_at[None, :]).astype(bf16)
    spread_at = jnp.arange(TRIAL_STATES * CELLS, dtype=jnp.int32) // CELLS
    spread_at = ((spread_at // trials) ^ me) * trials + spread_at % trials
    member_order = (spread_at[:, None] == jnp.arange(128, dtype=jnp.int32)[None, :]).astype(bf16)
    gram = pl.pallas_call(
        functools.partial(gram_kernel, trials),
        out_shape=jax.ShapeDtypeStruct((128, 128), f32),
        scratch_shapes=[pltpu.VMEM((total_rows, slots), bf16)],
        compiler_params=pltpu.CompilerParams(vmem_limit_bytes=VMEM_LIMIT),
    )(lax.dynamic_slice_in_dim(numbers, me * slots, slots, axis=1), fold, *observed)
    gram = total_of([gram] * members, swap)
    side = TRIAL_STATES * CELLS
    high, low = pl.pallas_call(
        transform_kernel,
        out_shape=[jax.ShapeDtypeStruct((side, side), bf16)] * 2,
        compiler_params=pltpu.CompilerParams(vmem_limit_bytes=VMEM_LIMIT),
    )(gram, member_order)
    high = high.reshape(members, trials * CELLS, side)
    low = low.reshape(members, trials * CELLS, side)

    analysis = jnp.zeros((trials, cells, VARS), bf16)
    pieces = [None] * members
    for q in order:
        mixed = mix(me ^ q, high, low, share_mean, parts)
        pieces[q] = lax.ppermute(mixed, "members", swap[q]) if q else mixed
    for q in range(members):
        analysis = lax.dynamic_update_slice_in_dim(analysis, pieces[q], (me ^ q) * share, axis=1)
    return analysis.reshape(trials, rows, cols, VARS)


def solution(mesh):
    placed = (
        P("members", "rows", "cols", None),
        P(("rows", "cols"), None),
        P(("rows", "cols"), None),
        P(("rows", "cols"), None),
        P(("rows", "cols"), None),
        P(("rows", "cols"), None),
        P(),
        P(),
    )
    return jax.shard_map(
        per_device,
        mesh=mesh,
        in_specs=placed,
        out_specs=P("members", "rows", "cols", None),
        check_vma=False,
    )
```

```python
import functools

import jax
import jax.numpy as jnp
from jax import lax
from jax.experimental import pallas as pl
from jax.experimental.pallas import tpu as pltpu
from jax.sharding import PartitionSpec as P

TRIAL_STATES = 80
FIELDS = 4
LEV = 32
SPECTRAL_BANDS = 16
BAND = 8
SHIFTS = 16
FP = 4
HW = 3
ITERS = 8
VARS = 128
CELLS = 8
CORNER = 16

bf16 = jnp.bfloat16
f32 = jnp.float32
HIGHEST = lax.Precision.HIGHEST
VMEM_LIMIT = 50 * 1024 * 1024
NT = (((1,), (1,)), ((), ()))


def shift_table(chan_base, band_weights):
    levels = jnp.arange(LEV, dtype=jnp.int32)
    shifts = jnp.arange(SHIFTS, dtype=jnp.int32)
    offset = levels[None, None, :] - (chan_base[None, :] + shifts[:, None])[:, :, None]
    total = jnp.zeros((SHIFTS, SPECTRAL_BANDS, FIELDS, LEV), f32)
    for layer in range(BAND):
        hit = offset == layer
        total = total + jnp.where(hit[:, :, None, :], band_weights[None, :, :, layer, None], 0.0)
    table = total.reshape(SHIFTS * SPECTRAL_BANDS, VARS)
    high = table.astype(bf16)
    low = (table - high.astype(f32)).astype(bf16)
    return jnp.concatenate([high, low], axis=1)


def obs_kernel(spots_ref, shift_ref, table_ref, own_ref, *refs):
    halo_refs, out_ref, spread = refs[:-2], refs[-2], refs[-1]
    slots = spots_ref.shape[0]
    cells = own_ref.shape[1] + sum(ref.shape[1] for ref in halo_refs)
    width = spread.shape[1]
    chunk = min(1024, slots)

    @pl.when(pl.program_id(0) == 0)
    def _():
        for start in range(0, slots, chunk):
            columns = lax.broadcasted_iota(jnp.int32, (chunk, width), 1)
            hits = jnp.zeros((chunk, width), f32)
            for q in range(FP):
                hits = hits + jnp.where(spots_ref[start:start + chunk, q:q + 1] == columns, 1.0 / FP, 0.0)
            spread[start:start + chunk, :] = hits.astype(bf16)

    panel = jnp.concatenate(
        [
            jnp.concatenate([own_ref[0], own_ref[1]], axis=1),
        ]
        + [jnp.concatenate([ref[0], ref[1]], axis=1) for ref in halo_refs]
        + [jnp.zeros((width - cells, 2 * VARS), bf16)] * (width > cells),
        axis=0,
    )
    for start in range(0, slots, chunk):
        average = jnp.dot(
            spread[start:start + chunk, :], panel, preferred_element_type=f32
        ).astype(bf16)
        shift = shift_ref[:, start:start + chunk]
        for k in range(2):
            part = average[:, k * VARS:(k + 1) * VARS]
            projected = lax.dot_general(
                table_ref[...],
                jnp.concatenate([part, part], axis=1),
                NT,
                preferred_element_type=f32,
            )
            picked = projected[:SPECTRAL_BANDS]
            for s in range(1, SHIFTS):
                picked = jnp.where(
                    shift == s, projected[s * SPECTRAL_BANDS:(s + 1) * SPECTRAL_BANDS], picked
                )
            out_ref[k, :, start:start + chunk] = picked.astype(out_ref.dtype)


def observe(spots, shifts, table, own, halo, pairs, dtype):
    slots = spots.shape[0]
    cells = own.shape[1] + sum(e.shape[1] for e in halo)
    width = cells + -cells % 256
    return pl.pallas_call(
        obs_kernel,
        grid=(pairs,),
        in_specs=[
            pl.BlockSpec((slots, FP), lambda i: (0, 0)),
            pl.BlockSpec((1, slots), lambda i: (0, 0)),
            pl.BlockSpec(table.shape, lambda i: (0, 0)),
        ]
        + [pl.BlockSpec((2, e.shape[1], VARS), lambda i: (i, 0, 0)) for e in [own] + halo],
        out_specs=pl.BlockSpec((2, SPECTRAL_BANDS, slots), lambda i: (i, 0, 0)),
        out_shape=jax.ShapeDtypeStruct((2 * pairs, SPECTRAL_BANDS, slots), dtype),
        scratch_shapes=[pltpu.VMEM((slots, width), bf16)],
        compiler_params=pltpu.CompilerParams(vmem_limit_bytes=VMEM_LIMIT),
        cost_estimate=pl.CostEstimate(
            flops=4 * pairs * slots * width * VARS,
            bytes_accessed=4 * pairs * width * VARS,
            transcendentals=0,
        ),
    )(spots, shifts, table, own, *halo)


def gram_kernel(trials, numbers_ref, fold_ref, *refs):
    obs_refs, out_ref, rows = refs[:-2], refs[-2], refs[-1]
    slots = numbers_ref.shape[1]
    root = jnp.sqrt(numbers_ref[SPECTRAL_BANDS:, :])
    size = trials * SPECTRAL_BANDS
    for q, ref in enumerate(obs_refs):
        obs = ref[:trials].astype(bf16).astype(f32)
        rows[q * size:(q + 1) * size, :] = (
            (obs * root[None]).reshape(size, slots).astype(bf16)
        )
    departure = (numbers_ref[:SPECTRAL_BANDS, :] - obs_refs[0][trials]) * root
    high = departure.astype(bf16)
    base = len(obs_refs) * size
    rows[base:base + SPECTRAL_BANDS, :] = high
    rows[base + SPECTRAL_BANDS:, :] = (departure - high.astype(f32)).astype(bf16)
    total_rows = rows.shape[0]
    folded = jnp.zeros((fold_ref.shape[0], total_rows), f32)
    edges = list(range(0, base, size)) + [base, total_rows]
    for start, end in zip(edges[:-1], edges[1:]):
        full = lax.dot_general(rows[start:end, :], rows[...], NT, preferred_element_type=f32)
        r = lax.broadcasted_iota(jnp.int32, full.shape, 0) & (SPECTRAL_BANDS - 1)
        c = lax.broadcasted_iota(jnp.int32, full.shape, 1) & (SPECTRAL_BANDS - 1)
        full = jnp.where(r == c, full, 0.0)
        high = full.astype(bf16)
        low = (full - high.astype(f32)).astype(bf16)
        fold = fold_ref[:, start:end]
        folded = folded + jnp.dot(fold, high, preferred_element_type=f32)
        folded = folded + jnp.dot(fold, low, preferred_element_type=f32)
    high = folded.astype(bf16)
    low = (folded - high.astype(f32)).astype(bf16)
    out_ref[...] = lax.dot_general(
        high, fold_ref[...], NT, preferred_element_type=f32
    ) + lax.dot_general(low, fold_ref[...], NT, preferred_element_type=f32)


def transform_kernel(gram_ref, order_ref, high_ref, low_ref):
    both = gram_ref[...]
    r = lax.broadcasted_iota(jnp.int32, both.shape, 0)
    c = lax.broadcasted_iota(jnp.int32, both.shape, 1)
    identity = jnp.where(r == c, 1.0, 0.0)
    inside = (r < TRIAL_STATES) & (c < TRIAL_STATES)
    gram = jnp.where(inside, both + (TRIAL_STATES - 1) * identity, 0.0)
    drive = jnp.where((r == TRIAL_STATES) & (c < TRIAL_STATES), both, 0.0)
    frobenius = jnp.sqrt(jnp.sum(gram * gram, keepdims=True))
    approach = gram / frobenius
    inverse = identity
    for sweep in range(ITERS):
        if sweep == 0:
            factor = 1.5 * identity - 0.5 * approach
            inverse = factor
        else:
            factor = 1.5 * identity - 0.5 * jnp.dot(inverse, approach, precision=HIGHEST)
            inverse = jnp.dot(factor, inverse, precision=HIGHEST)
        if sweep < ITERS - 1:
            approach = jnp.dot(approach, factor, precision=HIGHEST)
    weights = jnp.dot(jnp.dot(drive, inverse, precision=HIGHEST), inverse, precision=HIGHEST)
    weights = jnp.sum(weights, axis=0, keepdims=True) / frobenius
    coeff = jnp.sqrt((TRIAL_STATES - 1) / frobenius) * inverse + weights
    rows = TRIAL_STATES * CELLS
    r = lax.broadcasted_iota(jnp.int32, (rows, both.shape[1]), 0)
    c = lax.broadcasted_iota(jnp.int32, (rows, both.shape[1]), 1)
    expand = jnp.where(lax.shift_right_logical(r, 3) == c, 1.0, 0.0).astype(bf16)
    r = lax.broadcasted_iota(jnp.int32, (rows, rows), 0) & (CELLS - 1)
    c = lax.broadcasted_iota(jnp.int32, (rows, rows), 1) & (CELLS - 1)
    same = r == c
    high = coeff.astype(bf16)
    low = (coeff - high.astype(f32)).astype(bf16)
    for part, ref in ((high, high_ref), (low, low_ref)):
        tall = jnp.dot(expand, part, preferred_element_type=f32).astype(bf16)
        wide = lax.dot_general(tall, order_ref[...], NT, preferred_element_type=f32)
        ref[...] = jnp.where(same, wide, 0.0).astype(bf16)


def mix_kernel(dest_ref, high_ref, low_ref, mean_ref, *refs):
    parts, out_ref = refs[:-1], refs[-1]
    trials, cells = out_ref.shape[0], out_ref.shape[1]
    rounded = mean_ref[...].astype(bf16).astype(f32)
    for start in range(0, cells, 2 * CELLS):
        sides = []
        for half in range(2):
            block = [
                ref[:, start:start + 2 * CELLS, :]
                .astype(f32)[:, half * CELLS:(half + 1) * CELLS, :]
                .reshape(trials * CELLS, VARS)
                .astype(bf16)
                for ref in parts
            ]
            sides.append(jnp.concatenate(block, axis=0))
        x = jnp.concatenate(sides, axis=1)
        y = jnp.dot(high_ref[0], x, preferred_element_type=f32)
        y = y + jnp.dot(low_ref[0], x, preferred_element_type=f32)
        halves = [
            y[:, h * VARS:(h + 1) * VARS].reshape(trials, CELLS, VARS)
            + rounded[None, start + h * CELLS:start + (h + 1) * CELLS, :]
            for h in range(2)
        ]
        out_ref[:, start:start + 2 * CELLS, :] = jnp.concatenate(halves, axis=1).astype(bf16)


def mix(dest, high, low, mean, parts):
    trials, cells, _ = parts[0].shape
    block = min(64, cells)
    spec = pl.BlockSpec((trials, block, VARS), lambda i, d: (0, i, 0))
    kron_spec = pl.BlockSpec((1,) + high.shape[1:], lambda i, d: (d[0], 0, 0))
    return pl.pallas_call(
        mix_kernel,
        grid_spec=pltpu.PrefetchScalarGridSpec(
            num_scalar_prefetch=1,
            grid=(cells // block,),
            in_specs=[kron_spec, kron_spec, pl.BlockSpec((block, VARS), lambda i, d: (i, 0))]
            + [spec] * len(parts),
            out_specs=spec,
        ),
        out_shape=jax.ShapeDtypeStruct(parts[0].shape, bf16),
        compiler_params=pltpu.CompilerParams(vmem_limit_bytes=VMEM_LIMIT),
        cost_estimate=pl.CostEstimate(
            flops=4 * high.shape[1] * high.shape[2] * cells * VARS // CELLS,
            bytes_accessed=2 * (len(parts) + 1) * trials * cells * VARS,
            transcendentals=0,
        ),
    )(dest[None], high, low, mean, *parts)


def route(measured, rinv, obs_tile, footprint, obs_shift, tile_count, rows, cols):
    count = measured.shape[0]
    capacity = 2 * count // tile_count
    dest = obs_tile[:, 0]
    onehot = (jnp.arange(tile_count, dtype=jnp.int32)[:, None] == dest[None, :]).astype(bf16)
    lanes = 128
    groups = count // lanes
    grouped = onehot.reshape(tile_count, groups, lanes)
    upper = (jnp.arange(lanes)[:, None] < jnp.arange(lanes)[None, :]).astype(bf16)
    within = jnp.einsum("tbi,ij->tbj", grouped, upper, preferred_element_type=f32)
    sums = jnp.sum(grouped.astype(f32), axis=2)
    earlier = (jnp.arange(groups)[:, None] < jnp.arange(groups)[None, :]).astype(f32)
    offset = jnp.einsum("tb,bc->tc", sums, earlier, precision=HIGHEST)
    place = jnp.sum((within + offset[:, :, None]) * grouped.astype(f32), axis=0).reshape(count)
    slot = dest * capacity + place.astype(jnp.int32)
    wide = cols + 2 * HW
    i = footprint // wide
    j = footprint - i * wide
    ii, jj = i - HW, j - HW
    top = rows * cols
    bottom = top + HW * cols
    left = bottom + HW * cols
    right = left + HW * rows
    corner = right + HW * rows
    spot = ii * cols + jj
    spot = jnp.where(ii < 0, top + i * cols + jj, spot)
    spot = jnp.where(ii >= rows, bottom + (ii - rows) * cols + jj, spot)
    outer = jnp.where(ii < 0, i, HW + ii - rows)
    middle = (ii >= 0) & (ii < rows)
    at_left = jnp.where(middle, left + j * rows + ii, corner + j * CORNER + outer)
    at_right = jnp.where(
        middle,
        right + (jj - cols) * rows + ii,
        corner + (HW + jj - cols) * CORNER + outer,
    )
    spot = jnp.where(jj < 0, at_left, jnp.where(jj >= cols, at_right, spot))
    payload = jnp.concatenate(
        [
            measured.T.astype(bf16),
            rinv.T.astype(bf16),
            (spot >> 6).T.astype(bf16),
            (spot & 63).T.astype(bf16),
            obs_shift.T.astype(bf16),
            jnp.zeros((7, count), bf16),
        ],
        axis=0,
    )
    table = (slot[:, None] == jnp.arange(tile_count * capacity, dtype=jnp.int32)[None, :]).astype(bf16)
    packed = jnp.dot(payload, table, preferred_element_type=f32).astype(bf16)
    packed = packed.reshape(-1, tile_count, capacity).transpose(1, 0, 2)
    got = lax.all_to_all(packed, ("rows", "cols"), split_axis=0, concat_axis=0, tiled=True)
    got = got.transpose(1, 0, 2).reshape(-1, tile_count * capacity).astype(f32)
    numbers = got[:2 * SPECTRAL_BANDS]
    at = 2 * SPECTRAL_BANDS
    spots = (got[at:at + FP] * 64.0 + got[at + FP:at + 2 * FP]).astype(jnp.int32).T
    shifts = got[at + 2 * FP:at + 2 * FP + 1].astype(jnp.int32)
    return numbers, spots, shifts


def neighbours(x_last, x_first, axis):
    peers = lax.axis_size(axis)
    up = [(i, i + 1) for i in range(peers - 1)]
    down = [(i + 1, i) for i in range(peers - 1)]
    return lax.ppermute(x_last, axis, up), lax.ppermute(x_first, axis, down)


def total_of(pieces, swap):
    got = [lax.ppermute(p, "members", swap[q]) if q else p for q, p in enumerate(pieces)]
    total = got[0]
    for piece in got[1:]:
        total = total + piece
    return total


def per_device(
    ensemble, measured_brightness, obs_rinv, obs_tile, footprint, obs_shift, chan_base, band_weights
):
    trials, rows, cols, _ = ensemble.shape
    members = lax.axis_size("members")
    me = lax.axis_index("members")
    tile_count = lax.axis_size("rows") * lax.axis_size("cols")
    cells = rows * cols
    share = cells // members
    swap = [[(i, i ^ q) for i in range(members)] for q in range(members)]
    order = list(range(members - 1, -1, -1))

    local = jnp.sum(ensemble.astype(f32), axis=0).reshape(cells, VARS)
    share_mean = total_of(
        [lax.dynamic_slice_in_dim(local, (me ^ q) * share, share, axis=0) for q in range(members)],
        swap,
    ) / TRIAL_STATES
    mean = jnp.zeros((cells, VARS), f32)
    for q in range(members):
        piece = lax.ppermute(share_mean, "members", swap[q]) if q else share_mean
        mean = lax.dynamic_update_slice_in_dim(mean, piece, (me ^ q) * share, axis=0)
    mean = mean.reshape(rows, cols, VARS)
    rounded = mean.astype(bf16)

    numbers, spots, shifts = route(
        measured_brightness, obs_rinv, obs_tile, footprint, obs_shift, tile_count, rows, cols
    )
    table = shift_table(chan_base, band_weights)

    perturb = (ensemble.astype(f32) - mean[None]).astype(bf16)
    spare = (trials + 1) % 2
    stacked = jnp.concatenate(
        [perturb, rounded[None]] + [jnp.zeros((spare, rows, cols, VARS), bf16)] * (spare > 0), axis=0
    )
    count = stacked.shape[0]
    before, after = neighbours(stacked[:, rows - HW:], stacked[:, :HW], "rows")
    left, right = neighbours(
        stacked[:, :, cols - HW:].transpose(0, 2, 1, 3), stacked[:, :, :HW].transpose(0, 2, 1, 3), "cols"
    )

    def corners(at):
        both = jnp.concatenate([before[:, :, at:at + HW], after[:, :, at:at + HW]], axis=1)
        both = both.transpose(0, 2, 1, 3)
        return jnp.pad(both, ((0, 0), (0, 0), (0, CORNER - 2 * HW), (0, 0)))

    corner_left, corner_right = neighbours(corners(cols - HW), corners(0), "cols")
    halo = [
        e.reshape(count, -1, VARS) for e in (before, after, left, right, corner_left, corner_right)
    ]
    own = stacked.reshape(count, cells, VARS)

    flat = perturb.reshape(trials, cells, VARS)
    parts = [None] * members
    for q in order:
        piece = lax.dynamic_slice_in_dim(flat, (me ^ q) * share, share, axis=1)
        parts[q] = piece if q == 0 else lax.ppermute(piece, "members", swap[q])

    slots = spots.shape[0] // members
    observed = [None] * members
    for q in order:
        at = (me ^ q) * slots
        result = observe(
            lax.dynamic_slice_in_dim(spots, at, slots, axis=0),
            lax.dynamic_slice_in_dim(shifts, at, slots, axis=1),
            table,
            own,
            halo,
            (trials + 1) // 2 if q else (trials + 2) // 2,
            bf16 if q else f32,
        )
        observed[q] = lax.ppermute(result[:trials], "members", swap[q]) if q else result

    total_rows = (TRIAL_STATES + 2) * SPECTRAL_BANDS
    member_at = jnp.arange(total_rows, dtype=jnp.int32) // SPECTRAL_BANDS
    true_at = ((member_at // trials) ^ me) * trials + member_at % trials
    true_at = jnp.where(member_at >= TRIAL_STATES, TRIAL_STATES, true_at)
    fold = (jnp.arange(128, dtype=jnp.int32)[:, None] == true_at[None, :]).astype(bf16)
    spread_at = jnp.arange(TRIAL_STATES * CELLS, dtype=jnp.int32) // CELLS
    spread_at = ((spread_at // trials) ^ me) * trials + spread_at % trials
    member_order = (spread_at[:, None] == jnp.arange(128, dtype=jnp.int32)[None, :]).astype(bf16)
    gram = pl.pallas_call(
        functools.partial(gram_kernel, trials),
        out_shape=jax.ShapeDtypeStruct((128, 128), f32),
        scratch_shapes=[pltpu.VMEM((total_rows, slots), bf16)],
        compiler_params=pltpu.CompilerParams(vmem_limit_bytes=VMEM_LIMIT),
    )(lax.dynamic_slice_in_dim(numbers, me * slots, slots, axis=1), fold, *observed)
    gram = total_of([gram] * members, swap)
    side = TRIAL_STATES * CELLS
    high, low = pl.pallas_call(
        transform_kernel,
        out_shape=[jax.ShapeDtypeStruct((side, side), bf16)] * 2,
        compiler_params=pltpu.CompilerParams(vmem_limit_bytes=VMEM_LIMIT),
    )(gram, member_order)
    high = high.reshape(members, trials * CELLS, side)
    low = low.reshape(members, trials * CELLS, side)

    analysis = jnp.zeros((trials, cells, VARS), bf16)
    pieces = [None] * members
    for q in order:
        mixed = mix(me ^ q, high, low, share_mean, parts)
        pieces[q] = lax.ppermute(mixed, "members", swap[q]) if q else mixed
    for q in range(members):
        analysis = lax.dynamic_update_slice_in_dim(analysis, pieces[q], (me ^ q) * share, axis=1)
    return analysis.reshape(trials, rows, cols, VARS)


def solution(mesh):
    placed = (
        P("members", "rows", "cols", None),
        P(("rows", "cols"), None),
        P(("rows", "cols"), None),
        P(("rows", "cols"), None),
        P(("rows", "cols"), None),
        P(("rows", "cols"), None),
        P(),
        P(),
    )
    return jax.shard_map(
        per_device,
        mesh=mesh,
        in_specs=placed,
        out_specs=P("members", "rows", "cols", None),
        check_vma=False,
    )
```
